32 devices in a mesh: parts: 2 (over y), head: 16 (over z, x, core).
Axes of the slice: x: 2, y: 2, z: 4, core: 2. Of those that a mesh axis runs over, the one named last changes fastest.
Arguments:
- tokens: bfloat16 [512, 8192], P('parts', 'head'), parts along dimension 0, may hold values from -120 to 120
- pre_gain: bfloat16 [8192], P('head'), may hold values from 0.5 to 1.5
- w_in: bfloat16 [32, 256, 8192], P('head'), may hold values from -0.0625 to 0.0625
- w_dt: bfloat16 [32, 8192], P('head'), may hold values from -0.0625 to 0.0625
- dt_bias: float32 [32], P('head'), may hold values from -5 to -2
- a_log: float32 [32], P('head'), may hold values from -2.3 to 1.4
- conv_weight: bfloat16 [4, 32, 192], P(None, 'head'), may hold values from -3 to 3
- conv_bias: bfloat16 [32, 192], P('head'), may hold values from -2 to 2
- conv_tail: bfloat16 [6, 32, 192], P('parts', 'head'), parts along dimension 0, may hold values from -6 to 6
- init_state: float32 [64, 64, 256], P(('parts', 'head')), parts along dimension 0, may hold values from -0.6 to 0.6
- d_skip: float32 [32], P('head'), may hold values from 0.5 to 2
- norm_gain: bfloat16 [32, 64], P('head'), may hold values from 0.099609375 to 1.8984375
- w_out: bfloat16 [32, 64, 8192], P('head'), may hold values from -0.125 to 0.125
Outputs:
- mixer_out: bfloat16 [512, 8192], P('parts', 'head'), parts along dimension 0
- final_state: float32 [64, 64, 256], P(('parts', 'head')), parts along dimension 0
The draws below stay inside these ranges and needn't reach their ends.
There are 2 independent parts, one for each index of `parts`. The reference program is written for one: setup_inputs(seed, part) draws one part's arguments, and reference() takes and returns one part's arrays. A program takes and returns all parts, laid end to end along the dimension named above; an argument that names none is the same for every part. Nothing has to cross between parts.
All inputs are finite; a program needn't handle non-finite values.
Results may differ from the reference program's by a relative error of at most 0.0073.
Values may be sent and summed in bfloat16 or wider, within the bound.
A program may use at most 64 MiB of HBM per device.

```python
import math
import jax
import jax.numpy as jnp
from jax import lax

D = 8192
P_SIZE = 64
N = 256
G = 8
K = 4
TOKENS = 256
H = 32
NB = 64


def draw_tokens(key, part):
    key = jax.random.fold_in(key, 11)
    key_values, key_rows, key_cols = jax.random.split(key, 3)
    values = jax.random.truncated_normal(key_values, -4.0, 4.0, (TOKENS, D), jnp.float32)
    row_factor = jnp.exp(jax.random.uniform(key_rows, (TOKENS, 1), jnp.float32, 0.0, math.log(10.0)))
    rising = jnp.exp(math.log(3.0) * jnp.arange(D, dtype=jnp.float32) / max(D - 1, 1))
    col_factor = jnp.exp(jax.random.uniform(key_cols, (1, D), jnp.float32, 0.0, math.log(10.0))) * rising[None, :]
    return (values * row_factor * col_factor / 10.0).astype(jnp.bfloat16)


def block_levels(own_key, dims, shards, least, high):
    gain = 1.0
    for position, shards_of in shards:
        draws = jax.random.uniform(jax.random.fold_in(jax.random.fold_in(own_key, 6), position), (shards_of,), jnp.float32, least / len(shards), high / len(shards))
        gain = gain * jnp.repeat(jnp.exp(draws), dims[position] // shards_of).reshape((-1,) + (1,) * (len(dims) - 1 - position))
    return gain


def gaussian(key, dims, width, most, cuts=(), held_as=jnp.bfloat16):
    drawn = width * jax.random.normal(key, dims, jnp.float32)
    if cuts:
        drawn = drawn * block_levels(key, dims, cuts, -0.22, 0.18)
    return jnp.clip(drawn, -most, most).astype(held_as)


def setup_inputs(seed: int = 0, part: int = 0) -> dict:
    streams_of = jax.random.split(jax.random.key(seed), 14)
    own_keys = jax.random.split(jax.random.fold_in(streams_of[13], part), 14)
    tokens = draw_tokens(jax.random.fold_in(jax.random.fold_in(streams_of[13], part), 71), part)
    pre_gain = jnp.clip(1.0 + 0.1 * jax.random.normal(streams_of[1], (D,), jnp.float32), 0.5, 1.5).astype(jnp.bfloat16)
    w_in = gaussian(streams_of[2], (H, 2 * P_SIZE + 2 * NB, D), D ** -0.5, 0.0625, ((0, 16),))
    w_dt = gaussian(streams_of[3], (H, D), D ** -0.5, 0.0625, ((0, 16),))
    dt_bias = jnp.clip(-5.0 + 3.0 * jax.random.uniform(streams_of[4], (H,), jnp.float32) ** block_levels(streams_of[4], (H,), ((0, 16),), -0.2, 0.2), -5.0, -2.0)
    a_log = jnp.clip(-2.3 + 3.6999999 * jax.random.uniform(streams_of[5], (H,), jnp.float32) ** block_levels(streams_of[5], (H,), ((0, 16),), -0.2, 0.2), -2.3, 1.4)
    conv_weight = gaussian(streams_of[6], (K, H, P_SIZE + 2 * NB), 0.5, 3.0, ((1, 16),))
    conv_bias = gaussian(streams_of[7], (H, P_SIZE + 2 * NB), 0.3, 2.0, ((0, 16),))
    conv_tail = gaussian(own_keys[8], (K - 1, H, P_SIZE + 2 * NB), 1.0, 6.0, ((1, 16),))
    init_state = gaussian(own_keys[9], (H, P_SIZE, N), 0.1, 0.6, ((0, 16),), jnp.float32)
    d_skip = jnp.clip(0.5 + 1.5 * jax.random.uniform(streams_of[10], (H,), jnp.float32) ** block_levels(streams_of[10], (H,), ((0, 16),), -0.2, 0.2), 0.5, 2.0)
    norm_gain = jnp.clip(1.0 + 0.18 * jax.random.normal(streams_of[11], (H, P_SIZE), jnp.float32), 0.099609375, 1.8984375).astype(jnp.bfloat16)
    w_out = gaussian(streams_of[12], (H, P_SIZE, D), (H * P_SIZE) ** -0.5, 0.125, ((0, 16),))
    return dict(tokens=tokens, pre_gain=pre_gain, w_in=w_in, w_dt=w_dt, dt_bias=dt_bias, a_log=a_log, conv_weight=conv_weight, conv_bias=conv_bias, conv_tail=conv_tail, init_state=init_state, d_skip=d_skip, norm_gain=norm_gain, w_out=w_out)


epsilon = 1e-05

def reference(tokens, pre_gain, w_in, w_dt, dt_bias, a_log, conv_weight, conv_bias, conv_tail, init_state, d_skip, norm_gain, w_out):
    seq_len = tokens.shape[0]
    width_full = tokens.shape[1]
    head_count = w_in.shape[0]
    group_heads = head_count // G
    wide_tokens = tokens.astype(jnp.float32)
    row_scale = lax.rsqrt(lax.optimization_barrier(jnp.mean(wide_tokens * wide_tokens, axis=1, keepdims=True)) + epsilon)
    normed_in = (wide_tokens * row_scale * pre_gain.astype(jnp.float32)).astype(jnp.bfloat16)
    w_rows = w_in.reshape(-1, width_full)
    projected = lax.dot_general(normed_in, w_rows, (((1,), (1,)), ((), ())), preferred_element_type=jnp.float32)
    projected = projected.astype(jnp.bfloat16).reshape(seq_len, head_count, -1)
    dt_raw = jnp.dot(normed_in, w_dt.T, preferred_element_type=jnp.float32)
    conv_in = jnp.concatenate([conv_tail, projected[:, :, P_SIZE:]], axis=0).astype(jnp.float32)
    convolved = jnp.zeros((seq_len, head_count, P_SIZE + 2 * NB), jnp.float32) + conv_bias.astype(jnp.float32)
    for tap_index in range(K):
        convolved = convolved + conv_weight[tap_index].astype(jnp.float32) * conv_in[tap_index:tap_index + seq_len]
    activated = jax.nn.silu(convolved).astype(jnp.bfloat16)
    x_values = activated[:, :, :P_SIZE].astype(jnp.float32)
    b_slices = activated[:, :, P_SIZE:P_SIZE + NB].reshape(seq_len, G, group_heads * NB)
    c_slices = activated[:, :, P_SIZE + NB:].reshape(seq_len, G, group_heads * NB)
    b_heads = jnp.repeat(b_slices, group_heads, axis=1).astype(jnp.float32)
    c_heads = jnp.repeat(c_slices, group_heads, axis=1).astype(jnp.float32)
    dt_vals = jax.nn.softplus(dt_raw + dt_bias)
    decay_rate = -jnp.exp(a_log)
    rate_values = jnp.exp(dt_vals * decay_rate)
    drive_terms = dt_vals[:, :, None] * x_values

    def advance(carried, element):
        rate_now, drive_now, b_now, c_now = element
        carried = rate_now[:, None, None] * carried + drive_now[:, :, None] * b_now[:, None, :]
        return (carried, lax.optimization_barrier(jnp.sum(carried * c_now[:, None, :], axis=2)))
    final_state, outputs = lax.scan(advance, init_state.astype(jnp.float32), (rate_values, drive_terms, b_heads, c_heads))
    outputs = outputs + d_skip[None, :, None] * x_values
    gated_out = outputs * jax.nn.silu(projected[:, :, :P_SIZE].astype(jnp.float32))
    group_sq = lax.optimization_barrier(jnp.sum(gated_out * gated_out, axis=2)).reshape(seq_len, G, group_heads).sum(axis=2)
    inverse = lax.rsqrt(group_sq / (P_SIZE * group_heads) + epsilon)
    inverse_heads = jnp.repeat(inverse, group_heads, axis=1)
    normed_out = (gated_out * inverse_heads[:, :, None] * norm_gain.astype(jnp.float32)).astype(jnp.bfloat16)
    mixer_out = jnp.dot(normed_out.reshape(seq_len, -1), w_out.reshape(-1, width_full), preferred_element_type=jnp.float32)
    return (mixer_out.astype(jnp.bfloat16), final_state)
```

```python
import jax
import jax.numpy as jnp
from jax import lax
from jax.sharding import PartitionSpec as P

P_SIZE = 64
G = 8


epsilon = 1e-05


def from_partner(block, axis, apart):
    count = lax.axis_size(axis)
    route = []
    for low in range(count):
        high = low | 1 << apart
        if high != low and high < count:
            route += [(low, high), (high, low)]
    return lax.ppermute(block, axis, route)


def halves(values):
    high = values.astype(jnp.bfloat16)
    low = (values - lax.reduce_precision(values, 8, 7)).astype(jnp.bfloat16)
    return high, low


def stretch_scan(x_values, dt_vals, decay_rate, b_matrix, c_matrix, start_state):
    seq_len = x_values.shape[0]
    heads_here = x_values.shape[1]
    block_len = 128
    block_count = seq_len // block_len
    precise = lax.Precision.HIGHEST
    log_steps = (dt_vals * decay_rate[None, :]).reshape(block_count, block_len, heads_here)
    cumlog = jnp.cumsum(log_steps, axis=1)
    x_blocks = x_values.reshape(block_count, block_len, heads_here, -1)
    dt_blocks = dt_vals.reshape(block_count, block_len, heads_here)
    b_blocks = b_matrix.reshape(block_count, block_len, -1)
    c_blocks = c_matrix.reshape(block_count, block_len, -1)
    positions = jnp.arange(block_len)
    causal = (positions[:, None] >= positions[None, :])[None, :, :, None]
    log_gaps = cumlog[:, :, None, :] - cumlog[:, None, :, :]
    decays = jnp.where(causal, jnp.exp(jnp.where(causal, log_gaps, 0.0)), 0.0)
    scores = jnp.einsum("cin,cjn->cij", c_blocks, b_blocks, precision=precise)
    mixing = scores[:, :, :, None] * decays * dt_blocks[:, None, :, :]
    inner_part = jnp.einsum("cijh,cjhp->cihp", mixing, x_blocks, precision=precise)
    tail_decay = jnp.exp(cumlog[:, -1:, :] - cumlog) * dt_blocks
    local_states = jnp.einsum(
        "cjh,cjhp,cjn->chpn", tail_decay, x_blocks, b_blocks, precision=precise
    )
    totals = jnp.exp(cumlog[:, -1, :])

    def advance(carried, element):
        total_now, added = element
        return (total_now[:, None, None] * carried + added, carried)

    final_state, entering = lax.scan(advance, start_state, (totals, local_states))
    outer_part = jnp.einsum("cin,chpn->cihp", c_blocks, entering, precision=precise)
    outer_part = outer_part * jnp.exp(cumlog)[:, :, :, None]
    return ((inner_part + outer_part).reshape(seq_len, heads_here, -1), final_state)


def per_device(
    tokens,
    pre_gain,
    w_in,
    w_dt,
    dt_bias,
    a_log,
    conv_weight,
    conv_bias,
    conv_tail,
    init_state,
    d_skip,
    norm_gain,
    w_out,
):
    seq_len = tokens.shape[0]
    heads_here = w_in.shape[0]
    width_full = w_in.shape[2]
    w_flat = w_in.reshape(-1, width_full)
    contract_last = (((1,), (1,)), ((), ()))
    w_out_flat = w_out.reshape(-1, w_out.shape[2])
    w_columns = lax.all_to_all(w_out_flat, "head", split_axis=1, concat_axis=0, tiled=True)
    wide_tokens = tokens.astype(jnp.float32)
    gained = (wide_tokens * pre_gain.astype(jnp.float32)).astype(jnp.bfloat16)
    block_width = tokens.shape[1]
    shard_count = lax.axis_size("head")
    block_sq = jnp.sum(wide_tokens * wide_tokens, axis=1)
    sq_parts = jnp.stack(halves(block_sq)).reshape(-1)
    sq_rows = -(-sq_parts.shape[0] // block_width)
    sq_rows = -(-sq_rows // 16) * 16
    sq_block = jnp.pad(sq_parts, (0, sq_rows * block_width - sq_parts.shape[0]))
    payload = jnp.concatenate([gained, sq_block.reshape(sq_rows, block_width)], axis=0)
    gathered = lax.all_gather(payload, "head", axis=1, tiled=True)
    sq_all = gathered[seq_len:].astype(jnp.float32).reshape(sq_rows, shard_count, block_width)
    sq_all = jnp.sum(sq_all, axis=1).reshape(-1)
    row_sq = sq_all[:seq_len] + sq_all[seq_len : 2 * seq_len]
    row_scale = lax.rsqrt(row_sq / width_full + epsilon)[:, None]
    gained_full = gathered[:seq_len]
    proj_sum = row_scale * lax.dot_general(
        gained_full, w_flat, contract_last, preferred_element_type=jnp.float32
    )
    dt_raw = row_scale * lax.dot_general(
        gained_full, w_dt, contract_last, preferred_element_type=jnp.float32
    )
    projected = proj_sum.astype(jnp.bfloat16).reshape(seq_len, heads_here, -1)
    conv_in = jnp.concatenate([conv_tail, projected[:, :, P_SIZE:]], axis=0).astype(jnp.float32)
    convolved = jnp.zeros((seq_len,) + conv_bias.shape, jnp.float32) + conv_bias.astype(jnp.float32)
    for tap_index in range(conv_weight.shape[0]):
        convolved = (
            convolved
            + conv_weight[tap_index].astype(jnp.float32) * conv_in[tap_index : tap_index + seq_len]
        )
    activated = jax.nn.silu(convolved).astype(jnp.bfloat16)
    x_values = activated[:, :, :P_SIZE].astype(jnp.float32)
    group_span = lax.axis_size("head") // G
    my_index = lax.axis_index("head")
    own_maps = activated[:, :, P_SIZE:]
    for bit_number in range(group_span.bit_length() - 1):
        partner_maps = from_partner(own_maps, "head", bit_number)
        upper_half = my_index // (1 << bit_number) % 2 == 1
        own_maps = jnp.where(
            upper_half,
            jnp.concatenate([partner_maps, own_maps], axis=1),
            jnp.concatenate([own_maps, partner_maps], axis=1),
        )
    group_heads = own_maps.shape[1]
    slice_len = own_maps.shape[2] // 2
    b_matrix = own_maps[:, :, :slice_len].reshape(seq_len, -1).astype(jnp.float32)
    c_matrix = own_maps[:, :, slice_len:].reshape(seq_len, -1).astype(jnp.float32)
    dt_vals = jax.nn.softplus(dt_raw + dt_bias)
    decay_rate = -jnp.exp(a_log)
    outputs, final_state = stretch_scan(
        x_values, dt_vals, decay_rate, b_matrix, c_matrix, init_state
    )
    outputs = outputs + d_skip[None, :, None] * x_values
    gated_out = outputs * jax.nn.silu(projected[:, :, :P_SIZE].astype(jnp.float32))
    own_width = heads_here * P_SIZE
    gated_rows = jnp.concatenate(
        [
            gated_out.reshape(seq_len, own_width).astype(jnp.bfloat16),
            jnp.broadcast_to(norm_gain.reshape(1, own_width), (16, own_width)),
        ],
        axis=0,
    )
    gated_full = lax.all_gather(gated_rows, "head", axis=1, tiled=True).astype(jnp.float32)
    gains = gated_full[seq_len].reshape(G, -1)
    gated_groups = gated_full[:seq_len].reshape(seq_len, G, -1)
    group_sq = jnp.sum(gated_groups * gated_groups, axis=2, keepdims=True)
    inverse = lax.rsqrt(group_sq / (P_SIZE * group_heads) + epsilon)
    normed_out = (gated_groups * inverse * gains[None]).astype(jnp.bfloat16)
    mixer_out = jnp.dot(
        normed_out.reshape(seq_len, -1), w_columns, preferred_element_type=jnp.float32
    ).astype(jnp.bfloat16)
    return (mixer_out, final_state)


def solution(mesh):
    return jax.shard_map(
        per_device,
        mesh=mesh,
        in_specs=(
            P("parts", "head"),
            P("head"),
            P("head", None, None),
            P("head", None),
            P("head"),
            P("head"),
            P(None, "head", None),
            P("head", None),
            P("parts", "head", None),
            P(("parts", "head"), None, None),
            P("head"),
            P("head", None),
            P("head", None, None),
        ),
        out_specs=(P("parts", "head"), P(("parts", "head"), None, None)),
        check_vma=False,
    )
```

```python
import functools

import jax
import jax.numpy as jnp
from jax import lax
from jax.experimental import pallas as pl
from jax.experimental.pallas import tpu as pltpu
from jax.sharding import PartitionSpec as P

P_SIZE = 64
G = 8


epsilon = 1e-05


def from_partner(block, axis, apart):
    count = lax.axis_size(axis)
    route = []
    for low in range(count):
        high = low | 1 << apart
        if high != low and high < count:
            route += [(low, high), (high, low)]
    return lax.ppermute(block, axis, route)


def spread(depth, own_ref, full_ref, local_sem, send_sem, recv_sem):
    me = lax.axis_index("head")
    row, column, core = me // 4, (me // 2) % 2, me % 2
    width = own_ref.shape[1]
    across, beside = me + 2 - 4 * column, me + 1 - 2 * core
    has_upper, has_lower = row < depth - 1, row > 0

    def place(block):
        return full_ref.at[:, pl.ds(pl.multiple_of(block * width, 128), width)]

    def copy(block, way, target, source=None):
        return pltpu.make_async_remote_copy(
            src_ref=place(block) if source is None else source,
            dst_ref=place(block),
            send_sem=send_sem.at[way, block],
            recv_sem=recv_sem.at[block],
            device_id={"head": target},
            device_id_type=pl.DeviceIdType.MESH,
        )

    def arrived(block):
        copy(block, 3, beside).wait_recv()

    barrier = pltpu.get_barrier_semaphore()

    def greet(target):
        pl.semaphore_signal(
            barrier, inc=1, device_id={"head": target}, device_id_type=pl.DeviceIdType.MESH
        )

    greet(across)
    greet(beside)
    pl.when(has_upper)(lambda: greet(me + 4))
    pl.when(has_lower)(lambda: greet(me - 4))
    neighbours = 2 + has_upper.astype(jnp.int32) + has_lower.astype(jnp.int32)
    pl.semaphore_wait(barrier, neighbours)

    pl.when(has_upper)(lambda: copy(me, 0, me + 4, own_ref).start())
    pl.when(has_lower)(lambda: copy(me, 1, me - 4, own_ref).start())
    copy(me, 2, across, own_ref).start()
    copy(me, 3, beside, own_ref).start()
    keep = pltpu.make_async_copy(own_ref, place(me), local_sem)
    keep.start()

    def relay(block):
        arrived(block)
        copy(block, 3, beside).start()

    def from_lower(block):
        arrived(block)
        pl.when(has_upper)(lambda: copy(block, 0, me + 4).start())
        copy(block, 2, across).start()
        copy(block, 3, beside).start()

    def from_upper(block):
        arrived(block)
        pl.when(has_lower)(lambda: copy(block, 1, me - 4).start())
        copy(block, 2, across).start()
        copy(block, 3, beside).start()

    relay(across)
    for apart in range(1, depth):
        below, above = row - apart >= 0, row + apart < depth
        pl.when(below)(lambda: from_lower(me - 4 * apart))
        pl.when(above)(lambda: from_upper(me + 4 * apart))
        pl.when(below)(lambda: relay(across - 4 * apart))
        pl.when(above)(lambda: relay(across + 4 * apart))

    for level in range(depth):
        for side in range(2):
            arrived(level * 4 + side * 2 + 1 - core)
    for level in range(depth):
        own = level * 4 + column * 2 + core
        other = level * 4 + (1 - column) * 2 + core
        pl.when(has_upper & (level <= row))(lambda: copy(own, 0, me + 4, own_ref).wait_send())
        pl.when(has_lower & (level >= row))(lambda: copy(own, 1, me - 4, own_ref).wait_send())
        copy(own, 2, across, own_ref).wait_send()
        copy(own, 3, beside, own_ref).wait_send()
        copy(other, 3, beside, own_ref).wait_send()
    keep.wait()


def gather_columns(block, number):
    count = lax.axis_size("head")
    rows, width = block.shape
    if width % 128 or count % 4 or count > 16:
        return lax.all_gather(block, "head", axis=1, tiled=True)
    return pl.pallas_call(
        functools.partial(spread, count // 4),
        out_shape=jax.ShapeDtypeStruct((rows, width * count), block.dtype),
        in_specs=[pl.BlockSpec(memory_space=pl.ANY)],
        out_specs=pl.BlockSpec(memory_space=pl.ANY),
        scratch_shapes=[
            pltpu.SemaphoreType.DMA,
            pltpu.SemaphoreType.DMA((4, count)),
            pltpu.SemaphoreType.DMA((count,)),
        ],
        compiler_params=pltpu.CompilerParams(collective_id=number, has_side_effects=True),
        cost_estimate=pl.CostEstimate(
            flops=0, bytes_accessed=rows * width * count * 16, transcendentals=0
        ),
    )(block)


def halves(values):
    high = values.astype(jnp.bfloat16)
    low = (values - lax.reduce_precision(values, 8, 7)).astype(jnp.bfloat16)
    return high, low


def stretch_scan(x_values, dt_vals, decay_rate, b_matrix, c_matrix, start_state):
    seq_len = x_values.shape[0]
    heads_here = x_values.shape[1]
    block_len = 128
    block_count = seq_len // block_len
    precise = lax.Precision.HIGHEST
    log_steps = (dt_vals * decay_rate[None, :]).reshape(block_count, block_len, heads_here)
    cumlog = jnp.cumsum(log_steps, axis=1)
    x_blocks = x_values.reshape(block_count, block_len, heads_here, -1)
    dt_blocks = dt_vals.reshape(block_count, block_len, heads_here)
    b_blocks = b_matrix.reshape(block_count, block_len, -1)
    c_blocks = c_matrix.reshape(block_count, block_len, -1)
    positions = jnp.arange(block_len)
    causal = (positions[:, None] >= positions[None, :])[None, :, :, None]
    log_gaps = cumlog[:, :, None, :] - cumlog[:, None, :, :]
    decays = jnp.where(causal, jnp.exp(jnp.where(causal, log_gaps, 0.0)), 0.0)
    scores = jnp.einsum("cin,cjn->cij", c_blocks, b_blocks, precision=precise)
    mixing = scores[:, :, :, None] * decays * dt_blocks[:, None, :, :]
    inner_part = jnp.einsum("cijh,cjhp->cihp", mixing, x_blocks, precision=precise)
    tail_decay = jnp.exp(cumlog[:, -1:, :] - cumlog) * dt_blocks
    local_states = jnp.einsum(
        "cjh,cjhp,cjn->chpn", tail_decay, x_blocks, b_blocks, precision=precise
    )
    totals = jnp.exp(cumlog[:, -1, :])

    def advance(carried, element):
        total_now, added = element
        return (total_now[:, None, None] * carried + added, carried)

    final_state, entering = lax.scan(advance, start_state, (totals, local_states))
    outer_part = jnp.einsum("cin,chpn->cihp", c_blocks, entering, precision=precise)
    outer_part = outer_part * jnp.exp(cumlog)[:, :, :, None]
    return ((inner_part + outer_part).reshape(seq_len, heads_here, -1), final_state)


def per_device(
    tokens,
    pre_gain,
    w_in,
    w_dt,
    dt_bias,
    a_log,
    conv_weight,
    conv_bias,
    conv_tail,
    init_state,
    d_skip,
    norm_gain,
    w_out,
):
    seq_len = tokens.shape[0]
    heads_here = w_in.shape[0]
    width_full = w_in.shape[2]
    w_flat = w_in.reshape(-1, width_full)
    contract_last = (((1,), (1,)), ((), ()))
    w_out_flat = w_out.reshape(-1, w_out.shape[2])
    w_columns = lax.all_to_all(w_out_flat, "head", split_axis=1, concat_axis=0, tiled=True)
    wide_tokens = tokens.astype(jnp.float32)
    gained = (wide_tokens * pre_gain.astype(jnp.float32)).astype(jnp.bfloat16)
    block_width = tokens.shape[1]
    shard_count = lax.axis_size("head")
    block_sq = jnp.sum(wide_tokens * wide_tokens, axis=1)
    sq_parts = jnp.stack(halves(block_sq)).reshape(-1)
    sq_rows = -(-sq_parts.shape[0] // block_width)
    sq_rows = -(-sq_rows // 16) * 16
    sq_block = jnp.pad(sq_parts, (0, sq_rows * block_width - sq_parts.shape[0]))
    payload = jnp.concatenate([gained, sq_block.reshape(sq_rows, block_width)], axis=0)
    gathered = gather_columns(payload, 1)
    sq_all = gathered[seq_len:].astype(jnp.float32).reshape(sq_rows, shard_count, block_width)
    sq_all = jnp.sum(sq_all, axis=1).reshape(-1)
    row_sq = sq_all[:seq_len] + sq_all[seq_len : 2 * seq_len]
    row_scale = lax.rsqrt(row_sq / width_full + epsilon)[:, None]
    gained_full = gathered[:seq_len]
    proj_sum = row_scale * lax.dot_general(
        gained_full, w_flat, contract_last, preferred_element_type=jnp.float32
    )
    dt_raw = row_scale * lax.dot_general(
        gained_full, w_dt, contract_last, preferred_element_type=jnp.float32
    )
    projected = proj_sum.astype(jnp.bfloat16).reshape(seq_len, heads_here, -1)
    conv_in = jnp.concatenate([conv_tail, projected[:, :, P_SIZE:]], axis=0).astype(jnp.float32)
    convolved = jnp.zeros((seq_len,) + conv_bias.shape, jnp.float32) + conv_bias.astype(jnp.float32)
    for tap_index in range(conv_weight.shape[0]):
        convolved = (
            convolved
            + conv_weight[tap_index].astype(jnp.float32) * conv_in[tap_index : tap_index + seq_len]
        )
    activated = jax.nn.silu(convolved).astype(jnp.bfloat16)
    x_values = activated[:, :, :P_SIZE].astype(jnp.float32)
    group_span = lax.axis_size("head") // G
    my_index = lax.axis_index("head")
    own_maps = activated[:, :, P_SIZE:]
    for bit_number in range(group_span.bit_length() - 1):
        partner_maps = from_partner(own_maps, "head", bit_number)
        upper_half = my_index // (1 << bit_number) % 2 == 1
        own_maps = jnp.where(
            upper_half,
            jnp.concatenate([partner_maps, own_maps], axis=1),
            jnp.concatenate([own_maps, partner_maps], axis=1),
        )
    group_heads = own_maps.shape[1]
    slice_len = own_maps.shape[2] // 2
    b_matrix = own_maps[:, :, :slice_len].reshape(seq_len, -1).astype(jnp.float32)
    c_matrix = own_maps[:, :, slice_len:].reshape(seq_len, -1).astype(jnp.float32)
    dt_vals = jax.nn.softplus(dt_raw + dt_bias)
    decay_rate = -jnp.exp(a_log)
    outputs, final_state = stretch_scan(
        x_values, dt_vals, decay_rate, b_matrix, c_matrix, init_state
    )
    outputs = outputs + d_skip[None, :, None] * x_values
    gated_out = outputs * jax.nn.silu(projected[:, :, :P_SIZE].astype(jnp.float32))
    own_width = heads_here * P_SIZE
    gated_rows = jnp.concatenate(
        [
            gated_out.reshape(seq_len, own_width).astype(jnp.bfloat16),
            jnp.broadcast_to(norm_gain.reshape(1, own_width), (16, own_width)),
        ],
        axis=0,
    )
    gated_full = gather_columns(gated_rows, 2).astype(jnp.float32)
    gains = gated_full[seq_len].reshape(G, -1)
    gated_groups = gated_full[:seq_len].reshape(seq_len, G, -1)
    group_sq = jnp.sum(gated_groups * gated_groups, axis=2, keepdims=True)
    inverse = lax.rsqrt(group_sq / (P_SIZE * group_heads) + epsilon)
    normed_out = (gated_groups * inverse * gains[None]).astype(jnp.bfloat16)
    mixer_out = jnp.dot(
        normed_out.reshape(seq_len, -1), w_columns, preferred_element_type=jnp.float32
    ).astype(jnp.bfloat16)
    return (mixer_out, final_state)


def solution(mesh):
    return jax.shard_map(
        per_device,
        mesh=mesh,
        in_specs=(
            P("parts", "head"),
            P("head"),
            P("head", None, None),
            P("head", None),
            P("head"),
            P("head"),
            P(None, "head", None),
            P("head", None),
            P("parts", "head", None),
            P(("parts", "head"), None, None),
            P("head"),
            P("head", None),
            P("head", None, None),
        ),
        out_specs=(P("parts", "head"), P(("parts", "head"), None, None)),
        check_vma=False,
    )
```

```python
import functools

import jax
import jax.numpy as jnp
from jax import lax
from jax.experimental import pallas as pl
from jax.experimental.pallas import tpu as pltpu
from jax.sharding import PartitionSpec as P

P_SIZE = 64
G = 8


epsilon = 1e-05


def from_partner(block, axis, apart):
    count = lax.axis_size(axis)
    route = []
    for low in range(count):
        high = low | 1 << apart
        if high != low and high < count:
            route += [(low, high), (high, low)]
    return lax.ppermute(block, axis, route)


def spread(depth, own_ref, full_ref, local_sem, first_sem, send_sem, recv_sem):
    me = lax.axis_index("head")
    row, column, core = me // 4, (me // 2) % 2, me % 2
    count, width = 4 * depth, own_ref.shape[1]
    across, beside = me + 2 - 4 * column, me + 1 - 2 * core

    def place(block):
        return full_ref.at[:, pl.ds(pl.multiple_of(block * width, 128), width)]

    def copy(block, target, sent, source=None):
        return pltpu.make_async_remote_copy(
            src_ref=place(block) if source is None else source,
            dst_ref=place(block),
            send_sem=sent,
            recv_sem=recv_sem.at[block],
            device_id={"head": target},
            device_id_type=pl.DeviceIdType.MESH,
        )

    def relay_copy(block, way, source=None):
        return copy(block, (across, beside)[way], send_sem.at[way, block], source)

    def arrived(block):
        copy(block, beside, send_sem.at[1, block]).wait_recv()

    def along(start, step):
        return (start + 4 * step) % count

    barrier = pltpu.get_barrier_semaphore()
    peers = [along(me, step) for step in range(1, depth)]
    for target in [across, beside] + peers:
        pl.semaphore_signal(
            barrier, inc=1, device_id={"head": target}, device_id_type=pl.DeviceIdType.MESH
        )
    pl.semaphore_wait(barrier, depth + 1)

    firsts = [copy(me, peers[k], first_sem.at[k], own_ref) for k in range(depth - 1)]
    own_relays = [relay_copy(me, way, own_ref) for way in range(2)]
    for sent in own_relays + firsts:
        sent.start()
    keep = pltpu.make_async_copy(own_ref, place(me), local_sem)
    keep.start()

    relays = []

    def relay(block, ways):
        arrived(block)
        for way in ways:
            passed = relay_copy(block, way)
            passed.start()
            relays.append(passed)

    steps = sorted(range(1, depth), key=lambda step: min(step, depth - step))
    relay(across, (1,))
    for step in steps:
        relay(along(me, -step + depth), (0, 1))
    for step in steps:
        relay(along(across, -step + depth), (1,))
    for step in range(depth):
        arrived(along(beside, step))
        arrived(along(beside + 2 - 4 * column, step))
    for sent in firsts + own_relays + relays:
        sent.wait_send()
    keep.wait()


def gather_columns(block, number):
    count = lax.axis_size("head")
    rows, width = block.shape
    if width % 128 or count % 4 or count > 16:
        return lax.all_gather(block, "head", axis=1, tiled=True)
    return pl.pallas_call(
        functools.partial(spread, count // 4),
        out_shape=jax.ShapeDtypeStruct((rows, width * count), block.dtype),
        in_specs=[pl.BlockSpec(memory_space=pltpu.VMEM)],
        out_specs=pl.BlockSpec(memory_space=pltpu.VMEM),
        scratch_shapes=[
            pltpu.SemaphoreType.DMA,
            pltpu.SemaphoreType.DMA((count // 4,)),
            pltpu.SemaphoreType.DMA((2, count)),
            pltpu.SemaphoreType.DMA((count,)),
        ],
        compiler_params=pltpu.CompilerParams(
            collective_id=number, has_side_effects=True, vmem_limit_bytes=24 * 1024 * 1024
        ),
        cost_estimate=pl.CostEstimate(
            flops=0, bytes_accessed=rows * width * count * 16, transcendentals=0
        ),
    )(block)


def part_share(weights, shard_count, part_count):
    rows = weights.shape[0] // part_count
    share = lax.dynamic_slice_in_dim(weights, lax.axis_index("parts") * rows, rows, axis=0)
    blocks = share.reshape(rows, shard_count, -1).transpose(1, 0, 2)
    return blocks.reshape(shard_count * rows, -1)


def exchange_columns(share, shard_count, part_count):
    mine = lax.all_to_all(share, "head", split_axis=0, concat_axis=0, tiled=True)
    mine = mine.reshape(shard_count, -1, mine.shape[1])
    if part_count != 2:
        pieces = lax.all_gather(mine, "parts", axis=1)
    else:
        other = lax.ppermute(mine, "parts", [(0, 1), (1, 0)])
        first = lax.axis_index("parts") == 0
        pieces = jnp.stack(
            [jnp.where(first, mine, other), jnp.where(first, other, mine)], axis=1
        )
    return pieces.reshape(-1, mine.shape[2])


def finish(seq_len, gated_ref, weight_ref, out_ref):
    group_width = gated_ref.shape[1] // G
    total = jnp.zeros(out_ref.shape, jnp.float32)
    for group in range(G):
        span = pl.ds(group * group_width, group_width)
        gated = gated_ref[pl.ds(0, seq_len), span].astype(jnp.float32)
        gains = gated_ref[pl.ds(seq_len, 16), span].astype(jnp.float32)[:1]
        group_sq = jnp.sum(gated * gated, axis=1, keepdims=True)
        inverse = lax.rsqrt(group_sq / group_width + epsilon)
        normed = (gated * inverse * gains).astype(jnp.bfloat16)
        total = total + jnp.dot(
            normed, weight_ref[span, :], preferred_element_type=jnp.float32
        )
    out_ref[...] = total.astype(out_ref.dtype)


def halves(values):
    high = values.astype(jnp.bfloat16)
    low = (values - lax.reduce_precision(values, 8, 7)).astype(jnp.bfloat16)
    return high, low


def stretch_scan(x_values, dt_vals, decay_rate, b_matrix, c_matrix, start_state):
    seq_len = x_values.shape[0]
    heads_here = x_values.shape[1]
    block_len = 128
    block_count = seq_len // block_len
    precise = lax.Precision.HIGHEST
    log_steps = (dt_vals * decay_rate[None, :]).reshape(block_count, block_len, heads_here)
    cumlog = jnp.cumsum(log_steps, axis=1)
    x_blocks = x_values.reshape(block_count, block_len, heads_here, -1)
    dt_blocks = dt_vals.reshape(block_count, block_len, heads_here)
    b_blocks = b_matrix.reshape(block_count, block_len, -1)
    c_blocks = c_matrix.reshape(block_count, block_len, -1)
    positions = jnp.arange(block_len)
    causal = (positions[:, None] >= positions[None, :])[None, :, :, None]
    log_gaps = cumlog[:, :, None, :] - cumlog[:, None, :, :]
    decays = jnp.where(causal, jnp.exp(jnp.where(causal, log_gaps, 0.0)), 0.0)
    scores = jnp.einsum("cin,cjn->cij", c_blocks, b_blocks, precision=precise)
    mixing = scores[:, :, :, None] * decays * dt_blocks[:, None, :, :]
    inner_part = jnp.einsum("cijh,cjhp->cihp", mixing, x_blocks, precision=precise)
    tail_decay = jnp.exp(cumlog[:, -1:, :] - cumlog) * dt_blocks
    local_states = jnp.einsum(
        "cjh,cjhp,cjn->chpn", tail_decay, x_blocks, b_blocks, precision=precise
    )
    totals = jnp.exp(cumlog[:, -1, :])

    def advance(carried, element):
        total_now, added = element
        return (total_now[:, None, None] * carried + added, carried)

    final_state, entering = lax.scan(advance, start_state, (totals, local_states))
    outer_part = jnp.einsum("cin,chpn->cihp", c_blocks, entering, precision=precise)
    outer_part = outer_part * jnp.exp(cumlog)[:, :, :, None]
    return ((inner_part + outer_part).reshape(seq_len, heads_here, -1), final_state)


def per_device(
    tokens,
    pre_gain,
    w_in,
    w_dt,
    dt_bias,
    a_log,
    conv_weight,
    conv_bias,
    conv_tail,
    init_state,
    d_skip,
    norm_gain,
    w_out,
):
    seq_len = tokens.shape[0]
    heads_here = w_in.shape[0]
    width_full = w_in.shape[2]
    w_flat = w_in.reshape(-1, width_full)
    contract_last = (((1,), (1,)), ((), ()))
    shard_count = lax.axis_size("head")
    part_count = lax.axis_size("parts")
    w_share = part_share(w_out.reshape(-1, w_out.shape[2]), shard_count, part_count)
    wide_tokens = tokens.astype(jnp.float32)
    gained = (wide_tokens * pre_gain.astype(jnp.float32)).astype(jnp.bfloat16)
    block_width = tokens.shape[1]
    block_sq = jnp.sum(wide_tokens * wide_tokens, axis=1)
    sq_parts = jnp.stack(halves(block_sq)).reshape(-1)
    sq_rows = -(-sq_parts.shape[0] // block_width)
    sq_rows = -(-sq_rows // 16) * 16
    sq_block = jnp.pad(sq_parts, (0, sq_rows * block_width - sq_parts.shape[0]))
    payload = jnp.concatenate([gained, sq_block.reshape(sq_rows, block_width)], axis=0)
    gathered = gather_columns(payload, 1)
    gathered, w_share = lax.optimization_barrier((gathered, w_share))
    w_columns = exchange_columns(w_share, shard_count, part_count)
    sq_all = gathered[seq_len:].astype(jnp.float32).reshape(sq_rows, shard_count, block_width)
    sq_all = jnp.sum(sq_all, axis=1).reshape(-1)
    row_sq = sq_all[:seq_len] + sq_all[seq_len : 2 * seq_len]
    row_scale = lax.rsqrt(row_sq / width_full + epsilon)[:, None]
    gained_full = gathered[:seq_len]
    proj_sum = row_scale * lax.dot_general(
        gained_full, w_flat, contract_last, preferred_element_type=jnp.float32
    )
    dt_raw = row_scale * lax.dot_general(
        gained_full, w_dt, contract_last, preferred_element_type=jnp.float32
    )
    projected = proj_sum.astype(jnp.bfloat16).reshape(seq_len, heads_here, -1)
    conv_in = jnp.concatenate([conv_tail, projected[:, :, P_SIZE:]], axis=0).astype(jnp.float32)
    convolved = jnp.zeros((seq_len,) + conv_bias.shape, jnp.float32) + conv_bias.astype(jnp.float32)
    for tap_index in range(conv_weight.shape[0]):
        convolved = (
            convolved
            + conv_weight[tap_index].astype(jnp.float32) * conv_in[tap_index : tap_index + seq_len]
        )
    activated = jax.nn.silu(convolved).astype(jnp.bfloat16)
    x_values = activated[:, :, :P_SIZE].astype(jnp.float32)
    group_span = lax.axis_size("head") // G
    my_index = lax.axis_index("head")
    own_maps = activated[:, :, P_SIZE:]
    for bit_number in range(group_span.bit_length() - 1):
        partner_maps = from_partner(own_maps, "head", bit_number)
        upper_half = my_index // (1 << bit_number) % 2 == 1
        own_maps = jnp.where(
            upper_half,
            jnp.concatenate([partner_maps, own_maps], axis=1),
            jnp.concatenate([own_maps, partner_maps], axis=1),
        )
    slice_len = own_maps.shape[2] // 2
    b_matrix = own_maps[:, :, :slice_len].reshape(seq_len, -1).astype(jnp.float32)
    c_matrix = own_maps[:, :, slice_len:].reshape(seq_len, -1).astype(jnp.float32)
    dt_vals = jax.nn.softplus(dt_raw + dt_bias)
    decay_rate = -jnp.exp(a_log)
    outputs, final_state = stretch_scan(
        x_values, dt_vals, decay_rate, b_matrix, c_matrix, init_state
    )
    outputs = outputs + d_skip[None, :, None] * x_values
    gated_out = outputs * jax.nn.silu(projected[:, :, :P_SIZE].astype(jnp.float32))
    own_width = heads_here * P_SIZE
    gated_rows = jnp.concatenate(
        [
            gated_out.reshape(seq_len, own_width).astype(jnp.bfloat16),
            jnp.broadcast_to(norm_gain.reshape(1, own_width), (16, own_width)),
        ],
        axis=0,
    )
    gated_full = gather_columns(gated_rows, 2)
    mixer_out = pl.pallas_call(
        functools.partial(finish, seq_len),
        out_shape=jax.ShapeDtypeStruct((seq_len, w_columns.shape[1]), jnp.bfloat16),
        in_specs=[pl.BlockSpec(memory_space=pltpu.VMEM)] * 2,
        out_specs=pl.BlockSpec(memory_space=pltpu.VMEM),
        compiler_params=pltpu.CompilerParams(vmem_limit_bytes=40 * 1024 * 1024),
        cost_estimate=pl.CostEstimate(
            flops=2 * seq_len * w_columns.size,
            bytes_accessed=2 * w_columns.size,
            transcendentals=0,
        ),
    )(gated_full, w_columns)
    return (mixer_out, final_state)


def solution(mesh):
    return jax.shard_map(
        per_device,
        mesh=mesh,
        in_specs=(
            P("parts", "head"),
            P("head"),
            P("head", None, None),
            P("head", None),
            P("head"),
            P("head"),
            P(None, "head", None),
            P("head", None),
            P("parts", "head", None),
            P(("parts", "head"), None, None),
            P("head"),
            P("head", None),
            P("head", None, None),
        ),
        out_specs=(P("parts", "head"), P(("parts", "head"), None, None)),
        check_vma=False,
    )
```

```python
import functools

import jax
import jax.numpy as jnp
from jax import lax
from jax.experimental import pallas as pl
from jax.experimental.pallas import tpu as pltpu
from jax.sharding import PartitionSpec as P

P_SIZE = 64
G = 8


epsilon = 1e-05


def from_partner(block, axis, apart):
    count = lax.axis_size(axis)
    route = []
    for low in range(count):
        high = low | 1 << apart
        if high != low and high < count:
            route += [(low, high), (high, low)]
    return lax.ppermute(block, axis, route)


def spread(depth, own_ref, full_ref, local_sem, first_sem, send_sem, recv_sem):
    me = lax.axis_index("head")
    row, column, core = me // 4, (me // 2) % 2, me % 2
    count, width = 4 * depth, own_ref.shape[1]
    across, beside = me + 2 - 4 * column, me + 1 - 2 * core

    def place(block):
        return full_ref.at[:, pl.ds(pl.multiple_of(block * width, 128), width)]

    def copy(block, target, sent, source=None):
        return pltpu.make_async_remote_copy(
            src_ref=place(block) if source is None else source,
            dst_ref=place(block),
            send_sem=sent,
            recv_sem=recv_sem.at[block],
            device_id={"head": target},
            device_id_type=pl.DeviceIdType.MESH,
        )

    def relay_copy(block, way, source=None):
        return copy(block, (across, beside)[way], send_sem.at[way, block], source)

    def arrived(block):
        copy(block, beside, send_sem.at[1, block]).wait_recv()

    def along(start, step):
        return (start + 4 * step) % count

    barrier = pltpu.get_barrier_semaphore()
    peers = [along(me, step) for step in range(1, depth)]
    for target in [across, beside] + peers:
        pl.semaphore_signal(
            barrier, inc=1, device_id={"head": target}, device_id_type=pl.DeviceIdType.MESH
        )
    pl.semaphore_wait(barrier, depth + 1)

    firsts = [copy(me, peers[k], first_sem.at[k], own_ref) for k in range(depth - 1)]
    own_relays = [relay_copy(me, way, own_ref) for way in range(2)]
    for sent in own_relays + firsts:
        sent.start()
    keep = pltpu.make_async_copy(own_ref, place(me), local_sem)
    keep.start()

    relays = []

    def relay(block, ways):
        arrived(block)
        for way in ways:
            passed = relay_copy(block, way)
            passed.start()
            relays.append(passed)

    steps = sorted(range(1, depth), key=lambda step: min(step, depth - step))
    relay(across, (1,))
    for step in steps:
        relay(along(me, -step + depth), (0, 1))
    for step in steps:
        relay(along(across, -step + depth), (1,))
    for step in range(depth):
        arrived(along(beside, step))
        arrived(along(beside + 2 - 4 * column, step))
    for sent in firsts + own_relays + relays:
        sent.wait_send()
    keep.wait()


def spread_hops(depth, cuts, own_ref, full_ref, local_sem, send_sem, recv_sem):
    me = lax.axis_index("head")
    row, column, core = me // 4, (me // 2) % 2, me % 2
    width = own_ref.shape[1]
    across, beside = me + 2 - 4 * column, me + 1 - 2 * core
    has_upper, has_lower = row < depth - 1, row > 0

    def place(block, piece):
        rows = pl.ds(cuts[piece], cuts[piece + 1] - cuts[piece])
        return full_ref.at[rows, pl.ds(pl.multiple_of(block * width, 128), width)]

    def own_rows(piece):
        return own_ref.at[pl.ds(cuts[piece], cuts[piece + 1] - cuts[piece])]

    def copy(block, way, target, piece, own=False):
        return pltpu.make_async_remote_copy(
            src_ref=own_rows(piece) if own else place(block, piece),
            dst_ref=place(block, piece),
            send_sem=send_sem.at[way, piece, block],
            recv_sem=recv_sem.at[piece, block],
            device_id={"head": target},
            device_id_type=pl.DeviceIdType.MESH,
        )

    def arrived(block, piece):
        copy(block, 3, beside, piece).wait_recv()

    barrier = pltpu.get_barrier_semaphore()

    def greet(target):
        pl.semaphore_signal(
            barrier, inc=1, device_id={"head": target}, device_id_type=pl.DeviceIdType.MESH
        )

    greet(across)
    greet(beside)
    pl.when(has_upper)(lambda: greet(me + 4))
    pl.when(has_lower)(lambda: greet(me - 4))
    neighbours = 2 + has_upper.astype(jnp.int32) + has_lower.astype(jnp.int32)
    pl.semaphore_wait(barrier, neighbours)

    pieces = range(len(cuts) - 1)
    for piece in pieces:
        pl.when(has_upper)(lambda: copy(me, 0, me + 4, piece, True).start())
        pl.when(has_lower)(lambda: copy(me, 1, me - 4, piece, True).start())
        copy(me, 2, across, piece, True).start()
        copy(me, 3, beside, piece, True).start()
    mine = full_ref.at[:, pl.ds(pl.multiple_of(me * width, 128), width)]
    keep = pltpu.make_async_copy(own_ref, mine, local_sem)
    keep.start()

    def relay(block, piece):
        arrived(block, piece)
        copy(block, 3, beside, piece).start()

    def from_lower(block, piece):
        arrived(block, piece)
        pl.when(has_upper)(lambda: copy(block, 0, me + 4, piece).start())
        copy(block, 2, across, piece).start()
        copy(block, 3, beside, piece).start()

    def from_upper(block, piece):
        arrived(block, piece)
        pl.when(has_lower)(lambda: copy(block, 1, me - 4, piece).start())
        copy(block, 2, across, piece).start()
        copy(block, 3, beside, piece).start()

    for apart in range(1, depth):
        below, above = row - apart >= 0, row + apart < depth
        for piece in pieces:
            pl.when(below)(lambda: from_lower(me - 4 * apart, piece))
            pl.when(above)(lambda: from_upper(me + 4 * apart, piece))
            if apart == 1:
                relay(across, piece)
        for piece in pieces:
            if apart > 1:
                pl.when(row - apart + 1 >= 0)(lambda: relay(across - 4 * (apart - 1), piece))
                pl.when(row + apart - 1 < depth)(lambda: relay(across + 4 * (apart - 1), piece))
    for piece in pieces:
        pl.when(row - depth + 1 >= 0)(lambda: relay(across - 4 * (depth - 1), piece))
        pl.when(row + depth - 1 < depth)(lambda: relay(across + 4 * (depth - 1), piece))

    for piece in pieces:
        for level in range(depth):
            for side in range(2):
                arrived(level * 4 + side * 2 + 1 - core, piece)
        for level in range(depth):
            own = level * 4 + column * 2 + core
            other = level * 4 + (1 - column) * 2 + core
            pl.when(has_upper & (level <= row))(
                lambda: copy(own, 0, me + 4, piece, True).wait_send()
            )
            pl.when(has_lower & (level >= row))(
                lambda: copy(own, 1, me - 4, piece, True).wait_send()
            )
            copy(own, 2, across, piece, True).wait_send()
            copy(own, 3, beside, piece, True).wait_send()
            copy(other, 3, beside, piece, True).wait_send()
    keep.wait()


def gather_columns(block, number, pieces=0):
    count = lax.axis_size("head")
    rows, width = block.shape
    if width % 128 or count % 4 or count > 16:
        return lax.all_gather(block, "head", axis=1, tiled=True)
    cuts = [-(-rows * piece // (16 * max(pieces, 1))) * 16 for piece in range(pieces + 1)]
    kernel = functools.partial(spread, count // 4)
    sems = [(count // 4,), (2, count), (count,)]
    if pieces:
        kernel = functools.partial(spread_hops, count // 4, cuts)
        sems = [(4, pieces, count), (pieces, count)]
    return pl.pallas_call(
        kernel,
        out_shape=jax.ShapeDtypeStruct((rows, width * count), block.dtype),
        in_specs=[pl.BlockSpec(memory_space=pltpu.VMEM)],
        out_specs=pl.BlockSpec(memory_space=pltpu.VMEM),
        scratch_shapes=[pltpu.SemaphoreType.DMA]
        + [pltpu.SemaphoreType.DMA(sem) for sem in sems],
        compiler_params=pltpu.CompilerParams(
            collective_id=number, has_side_effects=True, vmem_limit_bytes=24 * 1024 * 1024
        ),
        cost_estimate=pl.CostEstimate(
            flops=0, bytes_accessed=rows * width * count * 16, transcendentals=0
        ),
    )(block)


def part_share(weights, shard_count, part_count):
    rows = weights.shape[0] // part_count
    share = lax.dynamic_slice_in_dim(weights, lax.axis_index("parts") * rows, rows, axis=0)
    blocks = share.reshape(rows, shard_count, -1).transpose(1, 0, 2)
    return blocks.reshape(shard_count * rows, -1)


def exchange_columns(share, shard_count, part_count):
    mine = lax.all_to_all(share, "head", split_axis=0, concat_axis=0, tiled=True)
    mine = mine.reshape(shard_count, -1, mine.shape[1])
    if part_count != 2:
        pieces = lax.all_gather(mine, "parts", axis=1)
    else:
        other = lax.ppermute(mine, "parts", [(0, 1), (1, 0)])
        first = lax.axis_index("parts") == 0
        pieces = jnp.stack(
            [jnp.where(first, mine, other), jnp.where(first, other, mine)], axis=1
        )
    return pieces.reshape(-1, mine.shape[2])


def finish(seq_len, gated_ref, weight_ref, out_ref):
    group_width = gated_ref.shape[1] // G
    total = jnp.zeros(out_ref.shape, jnp.float32)
    for group in range(G):
        span = pl.ds(group * group_width, group_width)
        gated = gated_ref[pl.ds(0, seq_len), span].astype(jnp.float32)
        gains = gated_ref[pl.ds(seq_len, 16), span].astype(jnp.float32)[:1]
        group_sq = jnp.sum(gated * gated, axis=1, keepdims=True)
        inverse = lax.rsqrt(group_sq / group_width + epsilon)
        normed = (gated * inverse * gains).astype(jnp.bfloat16)
        total = total + jnp.dot(
            normed, weight_ref[span, :], preferred_element_type=jnp.float32
        )
    out_ref[...] = total.astype(out_ref.dtype)


def halves(values):
    high = values.astype(jnp.bfloat16)
    low = (values - lax.reduce_precision(values, 8, 7)).astype(jnp.bfloat16)
    return high, low


def stretch_scan(x_values, dt_vals, decay_rate, b_matrix, c_matrix, start_state):
    seq_len = x_values.shape[0]
    heads_here = x_values.shape[1]
    block_len = 128
    block_count = seq_len // block_len
    precise = lax.Precision.HIGHEST
    log_steps = (dt_vals * decay_rate[None, :]).reshape(block_count, block_len, heads_here)
    cumlog = jnp.cumsum(log_steps, axis=1)
    x_blocks = x_values.reshape(block_count, block_len, heads_here, -1)
    dt_blocks = dt_vals.reshape(block_count, block_len, heads_here)
    b_blocks = b_matrix.reshape(block_count, block_len, -1)
    c_blocks = c_matrix.reshape(block_count, block_len, -1)
    positions = jnp.arange(block_len)
    causal = (positions[:, None] >= positions[None, :])[None, :, :, None]
    log_gaps = cumlog[:, :, None, :] - cumlog[:, None, :, :]
    decays = jnp.where(causal, jnp.exp(jnp.where(causal, log_gaps, 0.0)), 0.0)
    scores = jnp.einsum("cin,cjn->cij", c_blocks, b_blocks, precision=precise)
    mixing = scores[:, :, :, None] * decays * dt_blocks[:, None, :, :]
    inner_part = jnp.einsum("cijh,cjhp->cihp", mixing, x_blocks, precision=precise)
    tail_decay = jnp.exp(cumlog[:, -1:, :] - cumlog) * dt_blocks
    local_states = jnp.einsum(
        "cjh,cjhp,cjn->chpn", tail_decay, x_blocks, b_blocks, precision=precise
    )
    totals = jnp.exp(cumlog[:, -1, :])

    def advance(carried, element):
        total_now, added = element
        return (total_now[:, None, None] * carried + added, carried)

    final_state, entering = lax.scan(advance, start_state, (totals, local_states))
    outer_part = jnp.einsum("cin,chpn->cihp", c_blocks, entering, precision=precise)
    outer_part = outer_part * jnp.exp(cumlog)[:, :, :, None]
    return ((inner_part + outer_part).reshape(seq_len, heads_here, -1), final_state)


def per_device(
    tokens,
    pre_gain,
    w_in,
    w_dt,
    dt_bias,
    a_log,
    conv_weight,
    conv_bias,
    conv_tail,
    init_state,
    d_skip,
    norm_gain,
    w_out,
):
    seq_len = tokens.shape[0]
    heads_here = w_in.shape[0]
    width_full = w_in.shape[2]
    w_flat = w_in.reshape(-1, width_full)
    contract_last = (((1,), (1,)), ((), ()))
    shard_count = lax.axis_size("head")
    part_count = lax.axis_size("parts")
    w_share = part_share(w_out.reshape(-1, w_out.shape[2]), shard_count, part_count)
    wide_tokens = tokens.astype(jnp.float32)
    gained = (wide_tokens * pre_gain.astype(jnp.float32)).astype(jnp.bfloat16)
    block_width = tokens.shape[1]
    block_sq = jnp.sum(wide_tokens * wide_tokens, axis=1)
    sq_parts = jnp.stack(halves(block_sq)).reshape(-1)
    sq_rows = -(-sq_parts.shape[0] // block_width)
    sq_rows = -(-sq_rows // 16) * 16
    sq_block = jnp.pad(sq_parts, (0, sq_rows * block_width - sq_parts.shape[0]))
    payload = jnp.concatenate([gained, sq_block.reshape(sq_rows, block_width)], axis=0)
    gathered = gather_columns(payload, 1, 2)
    gathered, w_share = lax.optimization_barrier((gathered, w_share))
    w_columns = exchange_columns(w_share, shard_count, part_count)
    sq_all = gathered[seq_len:].astype(jnp.float32).reshape(sq_rows, shard_count, block_width)
    sq_all = jnp.sum(sq_all, axis=1).reshape(-1)
    row_sq = sq_all[:seq_len] + sq_all[seq_len : 2 * seq_len]
    row_scale = lax.rsqrt(row_sq / width_full + epsilon)[:, None]
    gained_full = gathered[:seq_len]
    proj_sum = row_scale * lax.dot_general(
        gained_full, w_flat, contract_last, preferred_element_type=jnp.float32
    )
    dt_raw = row_scale * lax.dot_general(
        gained_full, w_dt, contract_last, preferred_element_type=jnp.float32
    )
    projected = proj_sum.astype(jnp.bfloat16).reshape(seq_len, heads_here, -1)
    conv_in = jnp.concatenate([conv_tail, projected[:, :, P_SIZE:]], axis=0).astype(jnp.float32)
    convolved = jnp.zeros((seq_len,) + conv_bias.shape, jnp.float32) + conv_bias.astype(jnp.float32)
    for tap_index in range(conv_weight.shape[0]):
        convolved = (
            convolved
            + conv_weight[tap_index].astype(jnp.float32) * conv_in[tap_index : tap_index + seq_len]
        )
    activated = jax.nn.silu(convolved).astype(jnp.bfloat16)
    x_values = activated[:, :, :P_SIZE].astype(jnp.float32)
    group_span = lax.axis_size("head") // G
    my_index = lax.axis_index("head")
    own_maps = activated[:, :, P_SIZE:]
    for bit_number in range(group_span.bit_length() - 1):
        partner_maps = from_partner(own_maps, "head", bit_number)
        upper_half = my_index // (1 << bit_number) % 2 == 1
        own_maps = jnp.where(
            upper_half,
            jnp.concatenate([partner_maps, own_maps], axis=1),
            jnp.concatenate([own_maps, partner_maps], axis=1),
        )
    slice_len = own_maps.shape[2] // 2
    b_matrix = own_maps[:, :, :slice_len].reshape(seq_len, -1).astype(jnp.float32)
    c_matrix = own_maps[:, :, slice_len:].reshape(seq_len, -1).astype(jnp.float32)
    dt_vals = jax.nn.softplus(dt_raw + dt_bias)
    decay_rate = -jnp.exp(a_log)
    outputs, final_state = stretch_scan(
        x_values, dt_vals, decay_rate, b_matrix, c_matrix, init_state
    )
    outputs = outputs + d_skip[None, :, None] * x_values
    gated_out = outputs * jax.nn.silu(projected[:, :, :P_SIZE].astype(jnp.float32))
    own_width = heads_here * P_SIZE
    gated_rows = jnp.concatenate(
        [
            gated_out.reshape(seq_len, own_width).astype(jnp.bfloat16),
            jnp.broadcast_to(norm_gain.reshape(1, own_width), (16, own_width)),
        ],
        axis=0,
    )
    gated_full = gather_columns(gated_rows, 2)
    mixer_out = pl.pallas_call(
        functools.partial(finish, seq_len),
        out_shape=jax.ShapeDtypeStruct((seq_len, w_columns.shape[1]), jnp.bfloat16),
        in_specs=[pl.BlockSpec(memory_space=pltpu.VMEM)] * 2,
        out_specs=pl.BlockSpec(memory_space=pltpu.VMEM),
        compiler_params=pltpu.CompilerParams(vmem_limit_bytes=40 * 1024 * 1024),
        cost_estimate=pl.CostEstimate(
            flops=2 * seq_len * w_columns.size,
            bytes_accessed=2 * w_columns.size,
            transcendentals=0,
        ),
    )(gated_full, w_columns)
    return (mixer_out, final_state)


def solution(mesh):
    return jax.shard_map(
        per_device,
        mesh=mesh,
        in_specs=(
            P("parts", "head"),
            P("head"),
            P("head", None, None),
            P("head", None),
            P("head"),
            P("head"),
            P(None, "head", None),
            P("head", None),
            P("parts", "head", None),
            P(("parts", "head"), None, None),
            P("head"),
            P("head", None),
            P("head", None, None),
        ),
        out_specs=(P("parts", "head"), P(("parts", "head"), None, None)),
        check_vma=False,
    )
```
